128 devices in a mesh: row: 16 (over x, y), col: 8 (over z, core).
Axes of the slice: x: 4, y: 4, z: 4, core: 2. Of those that a mesh axis runs over, the one named last changes fastest.
Arguments:
- grad: bfloat16 [8192, 8192], P('row', 'col'), may hold values from -1 to 1
- old_basis: float32 [8192, 512], P('row'), may hold values from -1 to 1
- old_moments: float32 [512, 8192], P('row', 'col'), may hold values from -6 to 6
- owner_counts: int32 [16, 8], P('row'), may hold values from 1 to 8, 32 in all within a row
Outputs:
- new_basis: float32 [8192, 512], P(('row', 'col'))
- moments_owned: float32 [1024, 8192], P(('row', 'col'))
The draws below stay inside these ranges and needn't reach their ends.
Inputs may be any that keep to these rules, and one draw needn't show every extreme that they name: `owner_counts`: each row sums to 32; the largest entry of each row equals 8.
All inputs are finite; a program needn't handle non-finite values.
Results may differ from the reference program's by a relative error of at most 0.0003.
Values may be sent and summed in bfloat16 or wider, within the bound.
No kernel may reach another device: no remote copies, remote signals or barrier semaphores. Data moves between devices by JAX's collectives and lax.ppermute only.
A program may use at most 128 MiB of HBM per device.

```python
import math
import jax
import jax.numpy as jnp
import numpy as np
from jax import lax

M = 8192
N = 8192
R = 512
CAP = 8
N_ROW = 16
N_COL = 8


integer_variance = 56.0 / 3.0


def shared_left(key):
    spikes = min(64, R // 4)
    return jax.random.randint(key, (M, spikes), -7, 8).astype(jnp.float32)


def draw_grad(key, part):
    left_factor = shared_left(key)
    key = jax.random.fold_in(key, 11)
    spikes = left_factor.shape[1]
    right_key, noise_key = jax.random.split(key)
    right_factor = jax.random.randint(right_key, (N, spikes), -7, 8).astype(jnp.float32)
    groups = 3 * jnp.arange(spikes, dtype=jnp.int32) // spikes
    levels = jnp.where(groups == 0, 1.0, jnp.where(groups == 1, 0.5, 0.25)).astype(jnp.float32)
    lowrank = jnp.dot(left_factor * levels[None, :], right_factor.T, precision=lax.Precision.HIGHEST)
    strength = 40.0
    spread = 0.25
    jitter = jax.random.normal(noise_key, (M, N), jnp.float32)
    factor = spread * math.sqrt(strength) / (integer_variance * math.sqrt(M))
    return jnp.clip(factor * lowrank + spread * jitter, -1.0, 1.0).astype(jnp.bfloat16)


def draw_old_basis(key, part):
    left_factor = shared_left(key)
    key = jax.random.fold_in(key, 23)
    spikes = left_factor.shape[1]
    aligned_share = 0.9
    jitter = jax.random.normal(key, (M, R), jnp.float32)
    rest_share = math.sqrt(1.0 - aligned_share * aligned_share)
    aligned = aligned_share * left_factor / math.sqrt(integer_variance) + rest_share * jitter[:, :spikes]
    columns = jnp.concatenate([aligned, jitter[:, spikes:]], axis=1)
    return (columns / math.sqrt(M)).astype(jnp.float32)


def block_levels(key, dims, pieces, low, top_value):
    level, own = 1.0, jax.random.fold_in(key, 6)
    for axis_at, blocks in pieces:
        heights = jnp.exp(jax.random.uniform(jax.random.fold_in(own, axis_at), (blocks,), jnp.float32, low / len(pieces), top_value / len(pieces)))
        level = level * jnp.repeat(heights, dims[axis_at] // blocks).reshape([-1 if axis == axis_at else 1 for axis in range(len(dims))])
    return level


def profile(amount, total, most, lean):
    loads = [(1 << 20) // math.isqrt(standing ** lean) + 1 for standing in range(2, amount + 1)]
    surplus, holding = total - most - (amount - 1), [1] * (amount - 1)
    while surplus > 0:
        candidates = [i for i in range(amount - 1) if holding[i] < most]
        mass, budget = sum([loads[i] for i in candidates]), surplus
        for i in candidates:
            extra = min(most - holding[i], max(1, budget * loads[i] // mass), surplus)
            holding[i] = holding[i] + extra
            surplus = surplus - extra
    return np.array([most] + holding)


def ragged_sizes(own_key, count, total, reach, lean):
    if count == 2:
        one = jax.random.randint(own_key, (), max(1, total - reach), min(reach, total - 1) + 1)
        return jnp.stack([one, total - one])
    lengths = jnp.asarray(profile(count, total, reach, lean), jnp.int32)
    couples = (count - 1) // 2
    giver, receiver = lengths[1:1 + 2 * couples:2], lengths[2:2 + 2 * couples:2]
    slack = jnp.minimum(giver - 1, reach - receiver)
    passed = jax.random.randint(jax.random.fold_in(own_key, 1), (couples,), 0, 1 << 20) % (slack + 1)
    lengths = lengths.at[1:1 + 2 * couples:2].set(giver - passed).at[2:2 + 2 * couples:2].set(receiver + passed)
    return lengths[jax.random.permutation(jax.random.fold_in(own_key, 2), count)]


def scatter_about(stream_key, dims, scale, most, cuts=(), kind=jnp.bfloat16):
    array = jax.random.normal(stream_key, dims, jnp.float32) * scale
    if len(cuts) > 0:
        array = block_levels(stream_key, dims, cuts, -0.22, 0.18) * array
    return jnp.clip(array, min=-most, max=most).astype(kind)


def setup_inputs(seed: int = 0) -> dict:
    arg_keys = jax.random.split(jax.random.key(seed), 5)
    grad = draw_grad(jax.random.fold_in(arg_keys[4], 71), 0)
    old_basis = draw_old_basis(jax.random.fold_in(arg_keys[4], 71), 0)
    old_moments = scatter_about(arg_keys[2], (R, N), 1.0, 6.0, ((0, 16), (1, 8)), jnp.float32)
    owner_counts = jax.vmap(lambda own: ragged_sizes(own, N_COL, R // N_ROW, CAP, 2))(jax.random.split(arg_keys[3], N_ROW)).reshape((N_ROW, N_COL)).astype(jnp.int32)
    return dict(grad=grad, old_basis=old_basis, old_moments=old_moments, owner_counts=owner_counts)


highest = lax.Precision.HIGHEST

def orthonormal(image):
    cross = jnp.dot(image.T, image, precision=highest)
    lower = jnp.linalg.cholesky(cross)
    return lax.linalg.triangular_solve(lower, image, left_side=False, lower=True, transpose_a=True)

def reference(grad, old_basis, old_moments, owner_counts):
    dense = grad.astype(jnp.float32)
    basis = old_basis
    for step in range(2):
        projected = jnp.dot(dense.T, basis, precision=highest)
        image = jnp.dot(dense, projected, precision=highest)
        basis = orthonormal(image)
    rotation = jnp.dot(basis.T, old_basis, precision=highest)
    moved = jnp.dot(rotation, old_moments, precision=highest)
    groups = moved.reshape(N_ROW, R // N_ROW, N)
    starts = (jnp.cumsum(owner_counts, axis=1) - owner_counts).astype(jnp.int32)
    slots = jnp.arange(CAP, dtype=jnp.int32)
    index = starts[:, :, None] + slots[None, None, :]
    valid = slots[None, None, :] < owner_counts[:, :, None]
    index = jnp.clip(index, 0, R // N_ROW - 1).astype(jnp.int32)
    picked = jax.vmap(lambda block, rows: jnp.take(block, rows, axis=0))(groups, index)
    owned = jnp.where(valid[:, :, :, None], picked, jnp.float32(0.0))
    return (basis, owned.reshape(N_ROW * N_COL * CAP, N))
```

```python
import jax
import jax.numpy as jnp
from jax import lax
from jax.experimental import pallas as pl
from jax.experimental.pallas import tpu as pltpu
from jax.sharding import PartitionSpec as P

highest = lax.Precision.HIGHEST
f32 = jnp.float32
bf16 = jnp.bfloat16
BLOCK = 128
GROUP = 8


def invert_block(blk):
    lanes = lax.broadcasted_iota(jnp.int32, (GROUP, BLOCK), 1)
    subs = lax.broadcasted_iota(jnp.int32, (GROUP, BLOCK), 0)
    for g in range(BLOCK // GROUP):
        c = g * GROUP
        inside = (lanes >= c) & (lanes < c + GROUP)
        head = blk[c:c + GROUP, :]
        cols = [jnp.broadcast_to(head[:, c + j:c + j + 1], (GROUP, BLOCK)) for j in range(GROUP)]
        a = {}
        for j in range(GROUP):
            for i in range(j + 1):
                a[i, j] = jnp.broadcast_to(cols[j][i:i + 1, :], (GROUP, BLOCK))
        head = jnp.where(inside, jnp.where(lanes - c == subs, f32(1), f32(0)), head)
        rows = [jnp.broadcast_to(head[i:i + 1, :], (GROUP, BLOCK)) for i in range(GROUP)]
        ratio = {}
        scale = []
        for j in range(GROUP):
            scale.append(lax.rsqrt(a[j, j]))
            inv = scale[j] * scale[j]
            for k in range(j + 1, GROUP):
                ratio[j, k] = a[j, k] * inv
                for i in range(j + 1, k + 1):
                    a[i, k] = a[i, k] - ratio[j, i] * a[j, k]
        for j in range(GROUP):
            for k in range(j + 1, GROUP):
                rows[k] = rows[k] - ratio[j, k] * rows[j]
        rows = [rows[i] * scale[i] for i in range(GROUP)]
        out = rows[0]
        for i in range(1, GROUP):
            out = jnp.where(subs == i, rows[i], out)
        blk[c:c + GROUP, :] = out
        for t in range(g + 1, BLOCK // GROUP):
            low = blk[t * GROUP:(t + 1) * GROUP, :]
            col = [jnp.broadcast_to(low[:, c + j:c + j + 1], (GROUP, BLOCK)) for j in range(GROUP)]
            for j in range(GROUP):
                for k in range(j + 1, GROUP):
                    col[k] = col[k] - col[j] * ratio[j, k]
            acc = [col[j] * scale[j] * rows[j] for j in range(GROUP)]
            while len(acc) > 1:
                acc = [acc[i] + acc[i + 1] for i in range(0, len(acc), 2)]
            blk[t * GROUP:(t + 1) * GROUP, :] = jnp.where(inside, f32(0), low) - acc[0]


def factor_kernel(a_ref, out_ref, m_ref, blk):
    n = a_ref.shape[0]
    m_ref[...] = a_ref[...]
    out_ref[...] = jnp.zeros_like(out_ref)
    shape = (BLOCK, BLOCK)
    lower = lax.broadcasted_iota(jnp.int32, shape, 0) >= lax.broadcasted_iota(jnp.int32, shape, 1)
    dims = (((0,), (0,)), ((), ()))

    def mul(a, b):
        return jnp.dot(a, b, precision=highest, preferred_element_type=f32)

    def mul_t(a, b):
        return lax.dot_general(a, b, dims, precision=highest, preferred_element_type=f32)

    for o in range(0, n, BLOCK):
        e = o + BLOCK
        blk[...] = m_ref[o:e, o:e]
        invert_block(blk)
        x = jnp.where(lower, blk[...], f32(0))
        out_ref[o:e, o:e] = x
        if o > 0:
            left = mul(x, m_ref[o:e, :o])
            out_ref[o:e, :o] = left
        if e < n:
            right = mul(x, m_ref[o:e, e:])
            m_ref[e:, e:] -= mul_t(right, right)
            m_ref[e:, o:e] = -mul_t(right, x)
            if o > 0:
                m_ref[e:, :o] -= mul_t(right, left)


def inverse_factor(cross):
    n = cross.shape[0]
    return pl.pallas_call(
        factor_kernel,
        out_shape=jax.ShapeDtypeStruct((n, n), f32),
        in_specs=[pl.BlockSpec(memory_space=pltpu.VMEM)],
        out_specs=pl.BlockSpec(memory_space=pltpu.VMEM),
        scratch_shapes=[pltpu.VMEM((n, n), f32), pltpu.VMEM((BLOCK, BLOCK), f32)],
        compiler_params=pltpu.CompilerParams(vmem_limit_bytes=24 * 1024 * 1024),
    )(cross)


def parts(value):
    high = lax.reduce_precision(value, 8, 7)
    rest = value - high
    mid = lax.reduce_precision(rest, 8, 7)
    low = rest - mid
    return jnp.concatenate([high.astype(bf16), mid.astype(bf16), low.astype(bf16)], axis=1)


def times(left, right, dims):
    width = right.shape[1]
    wide = lax.dot_general(left, parts(right), (dims, ((), ())), preferred_element_type=f32)
    return wide[:, 2 * width:] + wide[:, width:2 * width] + wide[:, :width]


def body(grad, old_basis, old_moments, owner_counts):
    row_count = lax.axis_size("row")
    col_count = lax.axis_size("col")
    chips = col_count // 2
    col = lax.axis_index("col")
    core = col % 2
    depth = col // 2
    rank = old_basis.shape[1]
    half = rank // 2
    mate = [(i, i ^ 1) for i in range(col_count)]
    column = [[2 * z + c for z in range(chips)] for c in range(2)]
    layer = [[r * col_count + 2 * z + c for r in range(row_count) for z in range(chips)] for c in range(2)]

    def swap(value):
        return lax.ppermute(value, "col", mate)

    def both(value, axis):
        other = swap(value)
        first = jnp.where(core == 0, value, other)
        second = jnp.where(core == 0, other, value)
        return jnp.concatenate([first, second], axis=axis)

    def own(value, axis):
        size = value.shape[axis] // 2
        return lax.dynamic_slice_in_dim(value, core * size, size, axis)

    def exchange(value, kind):
        if kind == "plane":
            return lax.all_to_all(value, "row", split_axis=0, concat_axis=0, tiled=True)
        if kind == "column":
            return lax.all_to_all(value, "col", split_axis=0, concat_axis=0, tiled=True, axis_index_groups=column)
        return lax.all_to_all(value, ("row", "col"), split_axis=0, concat_axis=0, tiled=True, axis_index_groups=layer)

    def scatter_sum(value, kind, count):
        pieces = value.reshape((count, value.shape[0] // count) + value.shape[1:])
        return jnp.sum(exchange(pieces, kind), axis=0)

    def gather(value, kind, count):
        copies = jnp.broadcast_to(value[None], (count,) + value.shape)
        return exchange(copies, kind).reshape((count * value.shape[0],) + value.shape[1:])

    def total(value):
        rows, wide = value.shape
        split = jnp.concatenate([value[:, s:s + half] for s in range(0, wide, half)], axis=0)
        count = row_count * chips
        summed = gather(scatter_sum(split, "layer", count), "layer", count)
        joined = jnp.concatenate([summed[s:s + rows] for s in range(0, summed.shape[0], rows)], axis=1)
        return both(joined, 0)

    moments = lax.all_gather(old_moments, "row", axis=0, tiled=True)
    slab = both(grad, 1)

    def image_of(basis_half):
        projected = scatter_sum(times(slab, basis_half, ((0,), (0,))), "plane", row_count)
        projected = gather(projected, "plane", row_count)
        image = times(slab, projected, ((1,), (0,)))
        return both(scatter_sum(image, "column", chips), 1)

    image_one = image_of(own(old_basis, 1))
    cross_one = total(jnp.dot(own(image_one, 1).T, image_one, precision=highest))
    inverse_one = inverse_factor(cross_one)
    basis_one = jnp.dot(image_one, own(inverse_one, 0).T, precision=highest)
    image_two = image_of(gather(basis_one, "column", chips))
    share = image_two.shape[0]
    old_share = lax.dynamic_slice_in_dim(old_basis, depth * share, share, 0)
    pair = jnp.concatenate([image_two, old_share], axis=1)
    cross_pair = total(jnp.dot(own(image_two, 1).T, pair, precision=highest))
    inverse_two = inverse_factor(cross_pair[:, :rank])
    new_basis = jnp.dot(own(image_two, 0), inverse_two.T, precision=highest)

    moment_rows = old_moments.shape[0]
    mine = lax.dynamic_slice_in_dim(inverse_two, lax.axis_index("row") * moment_rows, moment_rows, 0)
    rotation = jnp.dot(mine, cross_pair[:, rank:], precision=highest)
    moved = jnp.dot(rotation, moments, precision=highest)
    counts = owner_counts[0]
    starts = jnp.cumsum(counts) - counts
    capacity = 2 * rank // (row_count * col_count)
    slots = jnp.arange(capacity, dtype=jnp.int32)
    index = jnp.clip(starts[:, None] + slots[None, :], 0, moment_rows - 1)
    valid = slots[None, :] < counts[:, None]
    outgoing = jnp.where(valid[:, :, None], jnp.take(moved, index, axis=0), f32(0.0))
    owned = lax.all_to_all(outgoing, "col", split_axis=0, concat_axis=2, tiled=True)
    return (new_basis, owned[0])


def solution(mesh):
    in_specs = (P("row", "col"), P("row", None), P("row", "col"), P("row", None))
    out_specs = (P(("row", "col"), None), P(("row", "col"), None))
    return jax.shard_map(body, mesh=mesh, in_specs=in_specs, out_specs=out_specs, check_vma=False)
```

```python
import functools
import itertools

import jax
import jax.numpy as jnp
from jax import lax
from jax.experimental import pallas as pl
from jax.experimental.pallas import tpu as pltpu
from jax.sharding import PartitionSpec as P

highest = lax.Precision.HIGHEST
f32 = jnp.float32
bf16 = jnp.bfloat16
BLOCK = 128
GROUP = 8


def invert_block(blk):
    lanes = lax.broadcasted_iota(jnp.int32, (GROUP, BLOCK), 1)
    subs = lax.broadcasted_iota(jnp.int32, (GROUP, BLOCK), 0)
    for g in range(BLOCK // GROUP):
        c = g * GROUP
        inside = (lanes >= c) & (lanes < c + GROUP)
        head = blk[c:c + GROUP, :]
        cols = [jnp.broadcast_to(head[:, c + j:c + j + 1], (GROUP, BLOCK)) for j in range(GROUP)]
        a = {}
        for j in range(GROUP):
            for i in range(j + 1):
                a[i, j] = jnp.broadcast_to(cols[j][i:i + 1, :], (GROUP, BLOCK))
        head = jnp.where(inside, jnp.where(lanes - c == subs, f32(1), f32(0)), head)
        rows = [jnp.broadcast_to(head[i:i + 1, :], (GROUP, BLOCK)) for i in range(GROUP)]
        ratio = {}
        scale = []
        for j in range(GROUP):
            scale.append(lax.rsqrt(a[j, j]))
            inv = scale[j] * scale[j]
            for k in range(j + 1, GROUP):
                ratio[j, k] = a[j, k] * inv
                for i in range(j + 1, k + 1):
                    a[i, k] = a[i, k] - ratio[j, i] * a[j, k]
        for j in range(GROUP):
            for k in range(j + 1, GROUP):
                rows[k] = rows[k] - ratio[j, k] * rows[j]
        rows = [rows[i] * scale[i] for i in range(GROUP)]
        out = rows[0]
        for i in range(1, GROUP):
            out = jnp.where(subs == i, rows[i], out)
        blk[c:c + GROUP, :] = out
        for t in range(g + 1, BLOCK // GROUP):
            low = blk[t * GROUP:(t + 1) * GROUP, :]
            col = [jnp.broadcast_to(low[:, c + j:c + j + 1], (GROUP, BLOCK)) for j in range(GROUP)]
            for j in range(GROUP):
                for k in range(j + 1, GROUP):
                    col[k] = col[k] - col[j] * ratio[j, k]
            acc = [col[j] * scale[j] * rows[j] for j in range(GROUP)]
            while len(acc) > 1:
                acc = [acc[i] + acc[i + 1] for i in range(0, len(acc), 2)]
            blk[t * GROUP:(t + 1) * GROUP, :] = jnp.where(inside, f32(0), low) - acc[0]


def mul(a, b):
    return jnp.dot(a, b, precision=highest, preferred_element_type=f32)


def mul_t(a, b):
    return lax.dot_general(a, b, (((0,), (0,)), ((), ())), precision=highest, preferred_element_type=f32)


def eliminate(m_ref, blk, first, last):
    n = m_ref.shape[0]
    shape = (BLOCK, BLOCK)
    lower = lax.broadcasted_iota(jnp.int32, shape, 0) >= lax.broadcasted_iota(jnp.int32, shape, 1)
    for o in range(first * BLOCK, last * BLOCK, BLOCK):
        e = o + BLOCK
        blk[...] = m_ref[o:e, o:e]
        invert_block(blk)
        x = jnp.where(lower, blk[...], f32(0))
        m_ref[o:e, o:e] = x
        if o > 0:
            left = mul(x, m_ref[o:e, :o])
            m_ref[o:e, :o] = left
        if e < n:
            right = mul(x, m_ref[o:e, e:])
            m_ref[o:e, e:] = jnp.zeros_like(right)
            m_ref[e:, e:] -= mul_t(right, right)
            m_ref[e:, o:e] = -mul_t(right, x)
            if o > 0:
                m_ref[e:, :o] -= mul_t(right, left)


def factor_kernel(first, last, a_ref, m_ref, blk):
    m_ref[...] = a_ref[...]
    eliminate(m_ref, blk, first, last)


def factor_step(value, first, last):
    n = value.shape[0]
    return pl.pallas_call(
        functools.partial(factor_kernel, first, last),
        out_shape=jax.ShapeDtypeStruct((n, n), f32),
        in_specs=[pl.BlockSpec(memory_space=pltpu.VMEM)],
        out_specs=pl.BlockSpec(memory_space=pltpu.VMEM),
        scratch_shapes=[pltpu.VMEM((BLOCK, BLOCK), f32)],
        compiler_params=pltpu.CompilerParams(vmem_limit_bytes=16 * 1024 * 1024),
        cost_estimate=pl.CostEstimate(flops=10_000_000_000, bytes_accessed=8 * n * n, transcendentals=0),
    )(value)


def factor_begin(cross):
    return factor_step(cross, 0, cross.shape[0] // BLOCK // 2)


def factor_end(value):
    blocks = value.shape[0] // BLOCK
    return factor_step(value, blocks // 2, blocks)


def tile_kernel(ids_ref, core_ref, own_ref, other_ref, out_ref):
    mine = ids_ref[pl.program_id(0)] // 8 == core_ref[0]

    @pl.when(mine)
    def _():
        out_ref[0] = own_ref[...]

    @pl.when(jnp.logical_not(mine))
    def _():
        out_ref[0] = other_ref[...]


def sorted_tiles(ids, core, own, other):
    rows = own.shape[0]
    tile = own.shape[1] // 8
    block = pl.BlockSpec((rows, tile), lambda t, ids, core: (0, ids[t] % 8))
    return pl.pallas_call(
        tile_kernel,
        out_shape=jax.ShapeDtypeStruct((4, rows, 4 * tile), own.dtype),
        grid_spec=pltpu.PrefetchScalarGridSpec(
            num_scalar_prefetch=2,
            grid=(16,),
            in_specs=[block, block],
            out_specs=pl.BlockSpec((1, rows, tile), lambda t, ids, core: (t // 4, 0, t % 4)),
        ),
        cost_estimate=pl.CostEstimate(flops=0, bytes_accessed=8 * own.size, transcendentals=0),
    )(ids, core.reshape(1), own, other)


def parts(value):
    high = lax.reduce_precision(value, 8, 7)
    rest = value - high
    mid = lax.reduce_precision(rest, 8, 7)
    low = rest - mid
    return jnp.concatenate([high.astype(bf16), mid.astype(bf16), low.astype(bf16)], axis=1)


def times(left, right, dims):
    width = right.shape[1]
    wide = lax.dot_general(left, parts(right), (dims, ((), ())), preferred_element_type=f32)
    return wide[:, 2 * width:] + wide[:, width:2 * width] + wide[:, :width]


def exact(left, right, dims):
    return lax.dot_general(left, right, (dims, ((), ())), precision=highest)


def after(value, earlier):
    return lax.optimization_barrier((value, earlier))


SIDE = 4


def body(grad, old_basis, old_moments, owner_counts):
    row_count = lax.axis_size("row")
    col_count = lax.axis_size("col")
    chips = col_count // 2
    row = lax.axis_index("row")
    col = lax.axis_index("col")
    core = col % 2
    depth = col // 2
    rank = old_basis.shape[1]
    half = rank // 2
    count = row_count * chips

    def place(x, y, z, c):
        return (x * SIDE + y) * col_count + 2 * z + c

    xs, ys, zs, cs = range(SIDE), range(SIDE), range(chips), range(2)

    groups = dict(
        column=[[place(x, y, z, c) for z in zs] for x in xs for y in ys for c in cs],
        plane=[[place(x, y, z, c) for x in xs for y in ys] for z in zs for c in cs],
        layer=[[place(x, y, z, c) for z in zs for x in xs for y in ys] for c in cs],
    )

    def moved_along(value, step, x_core):
        pairs = []
        for x, y, z, c in itertools.product(xs, ys, zs, cs):
            target = place((x + step) % SIDE, y, z, c) if c == x_core else place(x, (y + step) % SIDE, z, c)
            pairs.append((place(x, y, z, c), target))
        return lax.ppermute(value, ("row", "col"), pairs)

    def line_sum(pieces, x_core):
        far, near, back = [moved_along(pieces[d], d, x_core) for d in (2, 1, 3)]
        return pieces[0] + near + back + far

    def line_gather(value, x_core):
        far, near, back = [moved_along(value, -d, x_core) for d in (2, 1, 3)]
        return [value, near, far, back]

    def exchange(value, kind):
        return lax.all_to_all(value, ("row", "col"), split_axis=0, concat_axis=0, tiled=True, axis_index_groups=groups[kind])

    def swap(value):
        return lax.ppermute(value, "col", [(i, i ^ 1) for i in range(col_count)])

    def both(value, axis):
        other = swap(value)
        first = jnp.where(core == 0, value, other)
        second = jnp.where(core == 0, other, value)
        return jnp.concatenate([first, second], axis=axis)

    def own(value, axis):
        size = value.shape[axis] // 2
        return lax.dynamic_slice_in_dim(value, core * size, size, axis)

    def scatter_sum(value, kind):
        size = len(groups[kind][0])
        return jnp.sum(exchange(value.reshape((size, -1) + value.shape[1:]), kind), axis=0)

    def gather(value, kind):
        size = len(groups[kind][0])
        copies = jnp.broadcast_to(value[None], (size,) + value.shape)
        return exchange(copies, kind).reshape((-1,) + value.shape[1:])

    first_step, second_step = jnp.arange(SIDE * SIDE) // SIDE, jnp.arange(SIDE * SIDE) % SIDE
    x_step = jnp.where(core == 0, first_step, second_step)
    y_step = jnp.where(core == 0, second_step, first_step)
    tile_ids = (row // SIDE + x_step) % SIDE * SIDE + (row + y_step) % SIDE
    slab = sorted_tiles(tile_ids.astype(jnp.int32), core, grad, swap(grad))

    def outer_sum(value):
        return line_sum([times(slab[d], value, ((0,), (0,))) for d in range(SIDE)], 0)

    def inner_sum(value):
        return line_sum(list(value.reshape((SIDE, -1) + value.shape[1:])), 1)

    def image_of(share):
        chunks = line_gather(jnp.concatenate(line_gather(share, 1), axis=0), 0)
        terms = [times(slab[d], chunks[d], ((1,), (0,))) for d in (0, 1, 3, 2)]
        return scatter_sum(terms[0] + terms[1] + terms[2] + terms[3], "column")

    def halves(value):
        return value.reshape(count, -1, half)

    def joined(value):
        slices = gather(value, "layer").reshape(count, 2, -1, half)
        return jnp.concatenate([slices[:, 0].reshape(half, half), slices[:, 1].reshape(half, half)], axis=1)

    first = inner_sum(outer_sum(own(old_basis, 1)))
    image_rows = gather(image_of(first), "column")
    raw = outer_sum(image_rows)
    image_one = both(image_rows, 1)
    width = half // chips
    mine = lax.dynamic_slice_in_dim(image_rows, depth * width, width, 1)
    cross_one = exact(mine, image_one, ((0,), (0,)))
    cross_one = jnp.concatenate([cross_one[:, :half].reshape(row_count, -1, half), cross_one[:, half:].reshape(row_count, -1, half)], axis=1)
    cross_one = both(joined(jnp.sum(exchange(cross_one, "plane"), axis=0)), 0)
    raw, cross_one = after(raw, cross_one)
    inverse_one = factor_end(factor_begin(cross_one))
    raw = both(inner_sum(raw), 1)
    projected = exact(raw, own(inverse_one, 0), ((1,), (1,)))
    image_half = image_of(projected)
    moments = lax.all_gather(old_moments, "row", axis=0, tiled=True)
    image_half, moments = after(image_half, moments)
    image_two = both(image_half, 1)
    share = image_two.shape[0]
    old_share = lax.dynamic_slice_in_dim(old_basis, depth * share, share, 0)
    sums = [exact(image_half, v, ((0,), (0,))) for v in (image_two, old_share)]
    sums = jnp.concatenate([halves(v[:, s:s + half]) for v in sums for s in (0, half)], axis=1)
    sums = jnp.sum(exchange(sums, "layer"), axis=0)
    width = sums.shape[0] // 2
    cross_two = both(joined(sums[:width]), 0)
    sums, cross_two = after(sums, cross_two)
    inverse_two = factor_end(factor_begin(cross_two))
    cross_old = joined(sums[width:])
    cross_old, inverse_two = after(cross_old, inverse_two)
    cross_old = both(cross_old, 0)
    new_basis = exact(own(image_two, 0), inverse_two, ((1,), (1,)))

    moment_rows = old_moments.shape[0]
    mine = lax.dynamic_slice_in_dim(inverse_two, row * moment_rows, moment_rows, 0)
    rotation = jnp.dot(mine, cross_old, precision=highest)
    moved = jnp.dot(rotation, moments, precision=highest)
    counts = owner_counts[0]
    starts = jnp.cumsum(counts) - counts
    capacity = 2 * rank // (row_count * col_count)
    slots = jnp.arange(capacity, dtype=jnp.int32)
    index = jnp.clip(starts[:, None] + slots[None, :], 0, moment_rows - 1)
    valid = slots[None, :] < counts[:, None]
    outgoing = jnp.where(valid[:, :, None], jnp.take(moved, index, axis=0), f32(0.0))
    owned = lax.all_to_all(outgoing, "col", split_axis=0, concat_axis=2, tiled=True)
    return (new_basis, owned[0])


def solution(mesh):
    in_specs = (P("row", "col"), P("row", None), P("row", "col"), P("row", None))
    out_specs = (P(("row", "col"), None), P(("row", "col"), None))
    return jax.shard_map(body, mesh=mesh, in_specs=in_specs, out_specs=out_specs, check_vma=False)
```

```python
import functools
import itertools

import jax
import jax.numpy as jnp
from jax import lax
from jax.experimental import pallas as pl
from jax.experimental.pallas import tpu as pltpu
from jax.sharding import PartitionSpec as P

highest = lax.Precision.HIGHEST
f32 = jnp.float32
bf16 = jnp.bfloat16
BLOCK = 128
GROUP = 8


def invert_block(blk):
    lanes = lax.broadcasted_iota(jnp.int32, (GROUP, BLOCK), 1)
    subs = lax.broadcasted_iota(jnp.int32, (GROUP, BLOCK), 0)
    for g in range(BLOCK // GROUP):
        c = g * GROUP
        inside = (lanes >= c) & (lanes < c + GROUP)
        head = blk[c:c + GROUP, :]
        cols = [jnp.broadcast_to(head[:, c + j:c + j + 1], (GROUP, BLOCK)) for j in range(GROUP)]
        a = {}
        for j in range(GROUP):
            for i in range(j + 1):
                a[i, j] = jnp.broadcast_to(cols[j][i:i + 1, :], (GROUP, BLOCK))
        head = jnp.where(inside, jnp.where(lanes - c == subs, f32(1), f32(0)), head)
        rows = [jnp.broadcast_to(head[i:i + 1, :], (GROUP, BLOCK)) for i in range(GROUP)]
        ratio = {}
        scale = []
        for j in range(GROUP):
            scale.append(lax.rsqrt(a[j, j]))
            inv = scale[j] * scale[j]
            for k in range(j + 1, GROUP):
                ratio[j, k] = a[j, k] * inv
                for i in range(j + 1, k + 1):
                    a[i, k] = a[i, k] - ratio[j, i] * a[j, k]
        for j in range(GROUP):
            for k in range(j + 1, GROUP):
                rows[k] = rows[k] - ratio[j, k] * rows[j]
        rows = [rows[i] * scale[i] for i in range(GROUP)]
        out = rows[0]
        for i in range(1, GROUP):
            out = jnp.where(subs == i, rows[i], out)
        blk[c:c + GROUP, :] = out
        for t in range(g + 1, BLOCK // GROUP):
            low = blk[t * GROUP:(t + 1) * GROUP, :]
            col = [jnp.broadcast_to(low[:, c + j:c + j + 1], (GROUP, BLOCK)) for j in range(GROUP)]
            for j in range(GROUP):
                for k in range(j + 1, GROUP):
                    col[k] = col[k] - col[j] * ratio[j, k]
            acc = [col[j] * scale[j] * rows[j] for j in range(GROUP)]
            while len(acc) > 1:
                acc = [acc[i] + acc[i + 1] for i in range(0, len(acc), 2)]
            blk[t * GROUP:(t + 1) * GROUP, :] = jnp.where(inside, f32(0), low) - acc[0]


vmem = pl.BlockSpec(memory_space=pltpu.VMEM)


def local_params():
    return pltpu.CompilerParams(vmem_limit_bytes=16 * 1024 * 1024)


def mul(a, b):
    return jnp.dot(a, b, precision=highest, preferred_element_type=f32)


def mul_t(a, b):
    return lax.dot_general(a, b, (((0,), (0,)), ((), ())), precision=highest, preferred_element_type=f32)


def eliminate(m_ref, blk, first, last):
    n = m_ref.shape[0]
    shape = (BLOCK, BLOCK)
    lower = lax.broadcasted_iota(jnp.int32, shape, 0) >= lax.broadcasted_iota(jnp.int32, shape, 1)
    for o in range(first * BLOCK, last * BLOCK, BLOCK):
        e = o + BLOCK
        blk[...] = m_ref[o:e, o:e]
        invert_block(blk)
        x = jnp.where(lower, blk[...], f32(0))
        m_ref[o:e, o:e] = x
        if o > 0:
            left = mul(x, m_ref[o:e, :o])
            m_ref[o:e, :o] = left
        if e < n:
            right = mul(x, m_ref[o:e, e:])
            m_ref[o:e, e:] = jnp.zeros_like(right)
            m_ref[e:, e:] -= mul_t(right, right)
            m_ref[e:, o:e] = -mul_t(right, x)
            if o > 0:
                m_ref[e:, :o] -= mul_t(right, left)


def begin_kernel(core_ref, own_ref, other_ref, m_ref, blk):
    half = own_ref.shape[1]
    for side in range(2):
        columns = pl.ds(side * half, half)

        @pl.when(core_ref[0] == 0)
        def _(side=side, columns=columns):
            m_ref[:half, columns] = own_ref[side]
            m_ref[half:, columns] = other_ref[side]

        @pl.when(core_ref[0] != 0)
        def _(side=side, columns=columns):
            m_ref[:half, columns] = other_ref[side]
            m_ref[half:, columns] = own_ref[side]
    eliminate(m_ref, blk, 0, half // BLOCK)


def end_kernel(a_ref, m_ref, blk):
    n = a_ref.shape[0]
    m_ref[...] = a_ref[...]
    eliminate(m_ref, blk, n // BLOCK // 2, n // BLOCK)


def factor_call(kernel, n, in_specs):
    return pl.pallas_call(
        kernel,
        out_shape=jax.ShapeDtypeStruct((n, n), f32),
        in_specs=in_specs,
        out_specs=vmem,
        scratch_shapes=[pltpu.VMEM((BLOCK, BLOCK), f32)],
        compiler_params=local_params(),
        cost_estimate=pl.CostEstimate(flops=10_000_000_000, bytes_accessed=8 * n * n, transcendentals=0),
    )


def factor_begin(core, own, other):
    smem = pl.BlockSpec(memory_space=pltpu.SMEM)
    return factor_call(begin_kernel, 2 * own.shape[1], [smem, vmem, vmem])(core.reshape(1), own, other)


def factor_end(begun):
    return factor_call(end_kernel, begun.shape[0], [vmem])(begun)


def tile_kernel(ids_ref, core_ref, own_ref, other_ref, out_ref, turned_ref):
    tile = own_ref.shape[1] // 8
    for t in range(16):
        mine = ids_ref[t] // 8 == core_ref[0]
        source = pl.ds(pl.multiple_of(ids_ref[t] % 8 * tile, tile), tile)
        place = pl.ds(t % 4 * tile, tile)

        @pl.when(mine)
        def _(t=t, source=source, place=place):
            out_ref[t // 4, :, place] = own_ref[:, source]

        @pl.when(jnp.logical_not(mine))
        def _(t=t, source=source, place=place):
            out_ref[t // 4, :, place] = other_ref[:, source]
    for d in range(4):
        turned_ref[d] = out_ref[d].T


def sorted_tiles(ids, core, own, other):
    rows = own.shape[0]
    smem = pl.BlockSpec(memory_space=pltpu.SMEM)
    wide = own.shape[1] // 2
    return pl.pallas_call(
        tile_kernel,
        out_shape=(jax.ShapeDtypeStruct((4, rows, wide), own.dtype), jax.ShapeDtypeStruct((4, wide, rows), own.dtype)),
        in_specs=[smem, smem, vmem, vmem],
        out_specs=(vmem, vmem),
        compiler_params=local_params(),
        cost_estimate=pl.CostEstimate(flops=0, bytes_accessed=8 * own.size, transcendentals=0),
    )(ids, core.reshape(1), own, other)


def parts(value):
    high = value.astype(bf16)
    rest = value - high.astype(f32)
    mid = rest.astype(bf16)
    return high, mid, (rest - mid.astype(f32)).astype(bf16)


def times(left, terms):
    high, mid, low = [jnp.dot(left, term, preferred_element_type=f32) for term in terms]
    return low + mid + high


def pieces_kernel(left_ref, right_ref, *out_refs):
    terms = parts(right_ref[...])
    for d, out_ref in enumerate(out_refs):
        out_ref[...] = times(left_ref[d], terms)


def piece_products(left, right):
    shape = jax.ShapeDtypeStruct((left.shape[1], right.shape[1]), f32)
    flops = 6 * left.size * right.shape[1]
    return pl.pallas_call(
        pieces_kernel,
        out_shape=(shape,) * left.shape[0],
        in_specs=[vmem, vmem],
        out_specs=(vmem,) * left.shape[0],
        compiler_params=local_params(),
        cost_estimate=pl.CostEstimate(flops=flops, bytes_accessed=2 * left.size, transcendentals=0),
    )(left, right)


def chunk_kernel(first, chunks, *refs):
    left_ref, right_refs, rest = refs[0], refs[1:1 + chunks], refs[1 + chunks:]
    total = None if len(rest) == 1 else rest[0][...]
    for d, right_ref in enumerate(right_refs):
        term = times(left_ref[first + d], parts(right_ref[...]))
        total = term if total is None else total + term
    rest[-1][...] = total


def chunk_products(left, first, rights, total=None):
    shape = jax.ShapeDtypeStruct((left.shape[1], rights[0].shape[1]), f32)
    operands = [left, *rights] + ([] if total is None else [total])
    flops = 6 * len(rights) * left.shape[1] * left.shape[2] * shape.shape[1]
    return pl.pallas_call(
        functools.partial(chunk_kernel, first, len(rights)),
        out_shape=shape,
        in_specs=[vmem] * len(operands),
        out_specs=vmem,
        compiler_params=local_params(),
        cost_estimate=pl.CostEstimate(flops=flops, bytes_accessed=left.size, transcendentals=0),
    )(*operands)


def exact(left, right, dims):
    return lax.dot_general(left, right, (dims, ((), ())), precision=highest)


def after(value, earlier):
    return lax.optimization_barrier((value, earlier))


SIDE = 4


def body(grad, old_basis, old_moments, owner_counts):
    row_count = lax.axis_size("row")
    col_count = lax.axis_size("col")
    chips = col_count // 2
    row = lax.axis_index("row")
    col = lax.axis_index("col")
    core = col % 2
    depth = col // 2
    rank = old_basis.shape[1]
    half = rank // 2
    count = row_count * chips

    def place(x, y, z, c):
        return (x * SIDE + y) * col_count + 2 * z + c

    xs, ys, zs, cs = range(SIDE), range(SIDE), range(chips), range(2)

    groups = dict(
        column=[[place(x, y, z, c) for z in zs] for x in xs for y in ys for c in cs],
        plane=[[place(x, y, z, c) for x in xs for y in ys] for z in zs for c in cs],
        layer=[[place(x, y, z, c) for z in zs for x in xs for y in ys] for c in cs],
    )

    def moved_along(value, step, x_core):
        pairs = []
        for x, y, z, c in itertools.product(xs, ys, zs, cs):
            target = place((x + step) % SIDE, y, z, c) if c == x_core else place(x, (y + step) % SIDE, z, c)
            pairs.append((place(x, y, z, c), target))
        return lax.ppermute(value, ("row", "col"), pairs)

    def line_sum(pieces, x_core):
        far, near, back = [moved_along(pieces[d], d, x_core) for d in (2, 1, 3)]
        return pieces[0] + near + back + far

    def line_gather(value, x_core):
        far, near, back = [moved_along(value, -d, x_core) for d in (2, 1, 3)]
        return [value, near, far, back]

    def exchange(value, kind):
        return lax.all_to_all(value, ("row", "col"), split_axis=0, concat_axis=0, tiled=True, axis_index_groups=groups[kind])

    def swap(value):
        return lax.ppermute(value, "col", [(i, i ^ 1) for i in range(col_count)])

    def both(value, axis):
        other = swap(value)
        first = jnp.where(core == 0, value, other)
        second = jnp.where(core == 0, other, value)
        return jnp.concatenate([first, second], axis=axis)

    def own(value, axis):
        size = value.shape[axis] // 2
        return lax.dynamic_slice_in_dim(value, core * size, size, axis)

    def scatter_sum(value, kind):
        size = len(groups[kind][0])
        return jnp.sum(exchange(value.reshape((size, -1) + value.shape[1:]), kind), axis=0)

    def gather(value, kind):
        size = len(groups[kind][0])
        copies = jnp.broadcast_to(value[None], (size,) + value.shape)
        return exchange(copies, kind).reshape((-1,) + value.shape[1:])

    first_step, second_step = jnp.arange(SIDE * SIDE) // SIDE, jnp.arange(SIDE * SIDE) % SIDE
    x_step = jnp.where(core == 0, first_step, second_step)
    y_step = jnp.where(core == 0, second_step, first_step)
    tile_ids = (row // SIDE + x_step) % SIDE * SIDE + (row + y_step) % SIDE
    slab, slab_turned = sorted_tiles(tile_ids.astype(jnp.int32), core, grad, swap(grad))

    def outer_sum(value):
        return line_sum(piece_products(slab_turned, value), 0)

    def quarters(value):
        return list(value.reshape((SIDE, -1) + value.shape[1:]))

    def image_of(share):
        near = jnp.concatenate(line_gather(share, 1), axis=0)
        chunks = line_gather(near, 0)
        total = chunk_products(slab, 0, chunks[:1])
        total = chunk_products(slab, 2, chunks[2:3], total)
        total = chunk_products(slab, 1, chunks[1:2], total)
        total = chunk_products(slab, 3, chunks[3:], total)
        return scatter_sum(total, "column")

    def layer_sum(value):
        pieces = [value[:, s:s + half].reshape(count // 2, -1, half) for s in (0, half)]
        return jnp.sum(exchange(jnp.concatenate(pieces, axis=0), "layer"), axis=0)

    def joined(value):
        return gather(value, "layer").reshape(2, half, half)

    first = line_sum(quarters(outer_sum(own(old_basis, 1))), 1)
    image_rows = gather(image_of(first), "column")
    raw = outer_sum(image_rows)
    width = 2 * half // chips
    mine = lax.dynamic_slice_in_dim(image_rows, depth % 2 * width, width, 1)
    against = jnp.where(depth // 2 == core, image_rows, swap(image_rows))
    cross_one = exact(mine, against, ((0,), (0,))).reshape(row_count, -1, half)
    cross_one = joined(jnp.sum(exchange(cross_one, "plane"), axis=0))
    raw, cross_one = after(raw, cross_one)
    begun = factor_begin(core, cross_one, swap(cross_one))
    raw = quarters(raw)
    raw[0], begun = after(raw[0], begun)
    inverse_one = factor_end(begun)
    raw = both(line_sum(raw, 1), 1)
    projected = exact(raw, own(inverse_one, 0), ((1,), (1,)))
    cross_old = jnp.dot(inverse_one, both(jnp.concatenate([cross_one[0], cross_one[1]], axis=1), 0), precision=highest)
    image_half = image_of(projected)
    moments = lax.all_gather(old_moments, "row", axis=0, tiled=True)
    image_half, moments = after(image_half, moments)
    image_two = both(image_half, 1)
    cross_two = joined(layer_sum(exact(image_half, image_two, ((0,), (0,)))))
    cross_two, turned = after(cross_two, jnp.dot(cross_old, moments, precision=highest))
    inverse_two = factor_end(factor_begin(core, cross_two, swap(cross_two)))
    new_basis = exact(own(image_two, 0), inverse_two, ((1,), (1,)))

    moment_rows = old_moments.shape[0]
    mine = lax.dynamic_slice_in_dim(inverse_two, row * moment_rows, moment_rows, 0)
    moved = jnp.dot(mine, turned, precision=highest)
    counts = owner_counts[0]
    starts = jnp.cumsum(counts) - counts
    capacity = 2 * rank // (row_count * col_count)
    slots = jnp.arange(capacity, dtype=jnp.int32)
    index = jnp.clip(starts[:, None] + slots[None, :], 0, moment_rows - 1)
    valid = slots[None, :] < counts[:, None]
    outgoing = jnp.where(valid[:, :, None], jnp.take(moved, index, axis=0), f32(0.0))
    owned = lax.all_to_all(outgoing, "col", split_axis=0, concat_axis=2, tiled=True)
    return (new_basis, owned[0])


def solution(mesh):
    in_specs = (P("row", "col"), P("row", None), P("row", "col"), P("row", None))
    out_specs = (P(("row", "col"), None), P(("row", "col"), None))
    return jax.shard_map(body, mesh=mesh, in_specs=in_specs, out_specs=out_specs, check_vma=False)
```

```python
import functools
import itertools

import jax
import jax.numpy as jnp
from jax import lax
from jax.experimental import pallas as pl
from jax.experimental.pallas import tpu as pltpu
from jax.sharding import PartitionSpec as P

highest = lax.Precision.HIGHEST
f32 = jnp.float32
bf16 = jnp.bfloat16
BLOCK = 128
GROUP = 8
PANEL = 64


def leaf_scalars(blk, c):
    head = blk[c:c + GROUP, :]
    cols = [jnp.broadcast_to(head[:, c + j:c + j + 1], (GROUP, BLOCK)) for j in range(GROUP)]
    return {(i, j): jnp.broadcast_to(cols[j][i:i + 1, :], (GROUP, BLOCK)) for j in range(GROUP) for i in range(j + 1)}


def invert_block(blk):
    lanes = lax.broadcasted_iota(jnp.int32, (GROUP, BLOCK), 1)
    subs = lax.broadcasted_iota(jnp.int32, (GROUP, BLOCK), 0)
    later = None
    for g in range(BLOCK // GROUP):
        c = g * GROUP
        end = (c // PANEL + 1) * PANEL
        a = leaf_scalars(blk, c) if later is None else later
        later = leaf_scalars(blk, c + GROUP) if c + GROUP < end else None
        inside = (lanes >= c) & (lanes < c + GROUP)
        head = jnp.where(inside, jnp.where(lanes - c == subs, f32(1), f32(0)), blk[c:c + GROUP, :])
        rows = [jnp.broadcast_to(head[i:i + 1, :], (GROUP, BLOCK)) for i in range(GROUP)]
        low = {}
        scale = []
        for j in range(GROUP):
            scale.append(lax.rsqrt(a[j, j]))
            for k in range(j + 1, GROUP):
                low[j, k] = a[j, k] * scale[j]
            for k in range(j + 1, GROUP):
                for i in range(j + 1, k + 1):
                    a[i, k] = a[i, k] - low[j, i] * low[j, k]
            rows[j] = rows[j] * scale[j]
            for k in range(j + 1, GROUP):
                rows[k] = rows[k] - low[j, k] * rows[j]
        out = rows[0]
        for i in range(1, GROUP):
            out = jnp.where(subs == i, rows[i], out)
        blk[c:c + GROUP, :] = out
        for t in range(g + 1, end // GROUP):
            below = blk[t * GROUP:(t + 1) * GROUP, :]
            col = [jnp.broadcast_to(below[:, c + j:c + j + 1], (GROUP, BLOCK)) for j in range(GROUP)]
            for j in range(GROUP):
                col[j] = col[j] * scale[j]
                for k in range(j + 1, GROUP):
                    col[k] = col[k] - col[j] * low[j, k]
            if t == g + 1:
                for j in range(GROUP):
                    u = [jnp.broadcast_to(col[j][i:i + 1, :], (GROUP, BLOCK)) for i in range(GROUP)]
                    for q in range(GROUP):
                        for p in range(q + 1):
                            later[p, q] = later[p, q] - u[p] * u[q]
            terms = [col[j] * rows[j] for j in range(GROUP)]
            while len(terms) > 1:
                terms = [terms[i] + terms[i + 1] for i in range(0, len(terms), 2)]
            blk[t * GROUP:(t + 1) * GROUP, :] = jnp.where(inside, f32(0), below) - terms[0]
        if c + GROUP == end and end < BLOCK:
            start = end - PANEL
            done = blk[start:end, :]
            lane = lax.broadcasted_iota(jnp.int32, done.shape, 1)
            line = lax.broadcasted_iota(jnp.int32, done.shape, 0) + start
            ahead = (lane >= (line // GROUP + 1) * GROUP) & (lane < end)
            update = mul_t(done, jnp.where(ahead, f32(0), done))[end:, :]
            below = blk[end:, :]
            lane = lax.broadcasted_iota(jnp.int32, below.shape, 1)
            blk[end:, :] = jnp.where((lane >= start) & (lane < end), f32(0), below) - update


vmem = pl.BlockSpec(memory_space=pltpu.VMEM)


def local_params():
    return pltpu.CompilerParams(vmem_limit_bytes=16 * 1024 * 1024)


def mul(a, b):
    return jnp.dot(a, b, precision=highest, preferred_element_type=f32)


def mul_t(a, b):
    return lax.dot_general(a, b, (((0,), (0,)), ((), ())), precision=highest, preferred_element_type=f32)


def eliminate(m_ref, blk, first, last):
    n = m_ref.shape[0]
    shape = (BLOCK, BLOCK)
    lower = lax.broadcasted_iota(jnp.int32, shape, 0) >= lax.broadcasted_iota(jnp.int32, shape, 1)
    for o in range(first * BLOCK, last * BLOCK, BLOCK):
        e = o + BLOCK
        blk[...] = m_ref[o:e, o:e]
        invert_block(blk)
        x = jnp.where(lower, blk[...], f32(0))
        m_ref[o:e, o:e] = x
        if o > 0:
            left = mul(x, m_ref[o:e, :o])
            m_ref[o:e, :o] = left
        if e < n:
            right = mul(x, m_ref[o:e, e:])
            m_ref[o:e, e:] = jnp.zeros_like(right)
            m_ref[e:, e:] -= mul_t(right, right)
            m_ref[e:, o:e] = -mul_t(right, x)
            if o > 0:
                m_ref[e:, :o] -= mul_t(right, left)


def begin_kernel(core_ref, own_ref, other_ref, m_ref, blk):
    half = own_ref.shape[1]
    for side in range(2):
        columns = pl.ds(side * half, half)

        @pl.when(core_ref[0] == 0)
        def _(side=side, columns=columns):
            m_ref[:half, columns] = own_ref[side]
            m_ref[half:, columns] = other_ref[side]

        @pl.when(core_ref[0] != 0)
        def _(side=side, columns=columns):
            m_ref[:half, columns] = other_ref[side]
            m_ref[half:, columns] = own_ref[side]
    eliminate(m_ref, blk, 0, half // BLOCK)


def end_kernel(a_ref, m_ref, blk):
    n = a_ref.shape[0]
    m_ref[...] = a_ref[...]
    eliminate(m_ref, blk, n // BLOCK // 2, n // BLOCK)


def factor_call(kernel, n, in_specs):
    return pl.pallas_call(
        kernel,
        out_shape=jax.ShapeDtypeStruct((n, n), f32),
        in_specs=in_specs,
        out_specs=vmem,
        scratch_shapes=[pltpu.VMEM((BLOCK, BLOCK), f32)],
        compiler_params=local_params(),
        cost_estimate=pl.CostEstimate(flops=10_000_000_000, bytes_accessed=8 * n * n, transcendentals=0),
    )


def factor_begin(core, own, other):
    smem = pl.BlockSpec(memory_space=pltpu.SMEM)
    return factor_call(begin_kernel, 2 * own.shape[1], [smem, vmem, vmem])(core.reshape(1), own, other)


def factor_end(begun):
    return factor_call(end_kernel, begun.shape[0], [vmem])(begun)


def parts(value):
    high = value.astype(bf16)
    rest = value - high.astype(f32)
    mid = rest.astype(bf16)
    return high, mid, (rest - mid.astype(f32)).astype(bf16)


def times(left, terms):
    high, mid, low = [jnp.dot(left, term, preferred_element_type=f32) for term in terms]
    return low + mid + high


def pieces_kernel(left_ref, right_ref, *out_refs):
    terms = parts(right_ref[...])
    for d, out_ref in enumerate(out_refs):
        out_ref[...] = times(left_ref[d], terms)


def piece_products(left, right):
    shape = jax.ShapeDtypeStruct((left.shape[1], right.shape[1]), f32)
    flops = 6 * left.size * right.shape[1]
    return pl.pallas_call(
        pieces_kernel,
        out_shape=(shape,) * left.shape[0],
        in_specs=[vmem, vmem],
        out_specs=(vmem,) * left.shape[0],
        compiler_params=local_params(),
        cost_estimate=pl.CostEstimate(flops=flops, bytes_accessed=2 * left.size, transcendentals=0),
    )(left, right)


def setup_kernel(ids_ref, core_ref, own_ref, other_ref, basis_ref, slab_ref, turned_ref, *out_refs):
    tile = own_ref.shape[1] // 8
    half = basis_ref.shape[1] // 2
    terms = parts(basis_ref[:, pl.ds(pl.multiple_of(core_ref[0] * half, half), half)])
    for t in range(16):
        mine = ids_ref[t] // 8 == core_ref[0]
        source = pl.ds(pl.multiple_of(ids_ref[t] % 8 * tile, tile), tile)
        place = pl.ds(t % 4 * tile, tile)

        @pl.when(mine)
        def _(t=t, source=source, place=place):
            slab_ref[t // 4, :, place] = own_ref[:, source]

        @pl.when(jnp.logical_not(mine))
        def _(t=t, source=source, place=place):
            slab_ref[t // 4, :, place] = other_ref[:, source]
    for d in range(4):
        turned_ref[d] = slab_ref[d].T
        out_refs[d][...] = times(turned_ref[d], terms)


def set_up(ids, core, own, other, basis):
    rows = own.shape[0]
    wide, half = own.shape[1] // 2, basis.shape[1] // 2
    smem = pl.BlockSpec(memory_space=pltpu.SMEM)
    piece = jax.ShapeDtypeStruct((wide, half), f32)
    slabs = (jax.ShapeDtypeStruct((4, rows, wide), own.dtype), jax.ShapeDtypeStruct((4, wide, rows), own.dtype))
    slab, turned, *pieces = pl.pallas_call(
        setup_kernel,
        out_shape=slabs + (piece,) * 4,
        in_specs=[smem, smem, vmem, vmem, vmem],
        out_specs=(vmem,) * 6,
        compiler_params=local_params(),
        cost_estimate=pl.CostEstimate(flops=12 * own.size * half, bytes_accessed=8 * own.size, transcendentals=0),
    )(ids, core.reshape(1), own, other, basis)
    return slab, turned, pieces


def chunk_kernel(first, chunks, *refs):
    left_ref, right_refs, rest = refs[0], refs[1:1 + chunks], refs[1 + chunks:]
    total = None if len(rest) == 1 else rest[0][...]
    for d, right_ref in enumerate(right_refs):
        term = times(left_ref[first + d], parts(right_ref[...]))
        total = term if total is None else total + term
    rest[-1][...] = total


def chunk_products(left, first, rights, total=None):
    shape = jax.ShapeDtypeStruct((left.shape[1], rights[0].shape[1]), f32)
    operands = [left, *rights] + ([] if total is None else [total])
    flops = 6 * len(rights) * left.shape[1] * left.shape[2] * shape.shape[1]
    return pl.pallas_call(
        functools.partial(chunk_kernel, first, len(rights)),
        out_shape=shape,
        in_specs=[vmem] * len(operands),
        out_specs=vmem,
        compiler_params=local_params(),
        cost_estimate=pl.CostEstimate(flops=flops, bytes_accessed=left.size, transcendentals=0),
    )(*operands)


def exact(left, right, dims):
    return lax.dot_general(left, right, (dims, ((), ())), precision=highest)


def after(value, earlier):
    return lax.optimization_barrier((value, earlier))


SIDE = 4


def body(grad, old_basis, old_moments, owner_counts):
    row_count = lax.axis_size("row")
    col_count = lax.axis_size("col")
    chips = col_count // 2
    row = lax.axis_index("row")
    col = lax.axis_index("col")
    core = col % 2
    depth = col // 2
    rank = old_basis.shape[1]
    half = rank // 2
    count = row_count * chips

    def place(x, y, z, c):
        return (x * SIDE + y) * col_count + 2 * z + c

    xs, ys, zs, cs = range(SIDE), range(SIDE), range(chips), range(2)

    groups = dict(
        column=[[place(x, y, z, c) for z in zs] for x in xs for y in ys for c in cs],
        plane=[[place(x, y, z, c) for x in xs for y in ys] for z in zs for c in cs],
        layer=[[place(x, y, z, c) for z in zs for x in xs for y in ys] for c in cs],
    )

    def moved_along(value, step, x_core):
        pairs = []
        for x, y, z, c in itertools.product(xs, ys, zs, cs):
            target = place((x + step) % SIDE, y, z, c) if c == x_core else place(x, (y + step) % SIDE, z, c)
            pairs.append((place(x, y, z, c), target))
        return lax.ppermute(value, ("row", "col"), pairs)

    def line_sum(pieces, x_core):
        far, near, back = [moved_along(pieces[d], d, x_core) for d in (2, 1, 3)]
        return pieces[0] + near + back + far

    def line_gather(value, x_core):
        far, near, back = [moved_along(value, -d, x_core) for d in (2, 1, 3)]
        return [value, near, far, back]

    def exchange(value, kind):
        return lax.all_to_all(value, ("row", "col"), split_axis=0, concat_axis=0, tiled=True, axis_index_groups=groups[kind])

    def swap(value):
        return lax.ppermute(value, "col", [(i, i ^ 1) for i in range(col_count)])

    def both(value, axis):
        other = swap(value)
        first = jnp.where(core == 0, value, other)
        second = jnp.where(core == 0, other, value)
        return jnp.concatenate([first, second], axis=axis)

    def own(value, axis):
        size = value.shape[axis] // 2
        return lax.dynamic_slice_in_dim(value, core * size, size, axis)

    def scatter_sum(value, kind):
        size = len(groups[kind][0])
        return jnp.sum(exchange(value.reshape((size, -1) + value.shape[1:]), kind), axis=0)

    def gather(value, kind):
        size = len(groups[kind][0])
        copies = jnp.broadcast_to(value[None], (size,) + value.shape)
        return exchange(copies, kind).reshape((-1,) + value.shape[1:])

    first_step, second_step = jnp.arange(SIDE * SIDE) // SIDE, jnp.arange(SIDE * SIDE) % SIDE
    x_step = jnp.where(core == 0, first_step, second_step)
    y_step = jnp.where(core == 0, second_step, first_step)
    tile_ids = (row // SIDE + x_step) % SIDE * SIDE + (row + y_step) % SIDE
    slab, slab_turned, pieces = set_up(tile_ids.astype(jnp.int32), core, grad, swap(grad), old_basis)

    def quarters(value):
        return list(value.reshape((SIDE, -1) + value.shape[1:]))

    def image_of(share):
        near = jnp.concatenate(line_gather(share, 1), axis=0)
        chunks = line_gather(near, 0)
        total = chunk_products(slab, 0, chunks[:1])
        total = chunk_products(slab, 2, chunks[2:3], total)
        total = chunk_products(slab, 1, chunks[1:2], total)
        return chunk_products(slab, 3, chunks[3:], total)

    def layer_sum(value):
        pieces = [value[:, s:s + half].reshape(count // 2, -1, half) for s in (0, half)]
        return jnp.sum(exchange(jnp.concatenate(pieces, axis=0), "layer"), axis=0)

    def joined(value):
        return gather(value, "layer").reshape(2, half, half)

    first = line_sum(quarters(line_sum(pieces, 0)), 1)
    image_rows = gather(scatter_sum(image_of(first), "column"), "column")
    raw = line_sum(piece_products(slab_turned, image_rows), 0)
    width = 2 * half // chips
    mine = lax.dynamic_slice_in_dim(image_rows, depth % 2 * width, width, 1)
    against = jnp.where(depth // 2 == core, image_rows, swap(image_rows))
    cross_one = exact(mine, against, ((0,), (0,))).reshape(row_count, -1, half)
    cross_one = joined(jnp.sum(exchange(cross_one, "plane"), axis=0))
    raw, cross_one = after(raw, cross_one)
    begun = factor_begin(core, cross_one, swap(cross_one))
    raw = quarters(raw)
    raw[0], begun = after(raw[0], begun)
    inverse_one = factor_end(begun)
    raw = both(line_sum(raw, 1), 1)
    projected = exact(raw, own(inverse_one, 0), ((1,), (1,)))
    cross_old = jnp.dot(inverse_one, both(jnp.concatenate([cross_one[0], cross_one[1]], axis=1), 0), precision=highest)
    image_half, cross_old = after(image_of(projected), cross_old)
    image_half = scatter_sum(image_half, "column")
    moments = lax.all_gather(old_moments, "row", axis=0, tiled=True)
    image_half, moments = after(image_half, moments)
    image_two = both(image_half, 1)
    cross_two = joined(layer_sum(exact(image_half, image_two, ((0,), (0,)))))
    cross_two, turned = after(cross_two, jnp.dot(cross_old, moments, precision=highest))
    inverse_two = factor_end(factor_begin(core, cross_two, swap(cross_two)))
    new_basis = exact(own(image_two, 0), inverse_two, ((1,), (1,)))

    moment_rows = old_moments.shape[0]
    mine = lax.dynamic_slice_in_dim(inverse_two, row * moment_rows, moment_rows, 0)
    moved = jnp.dot(mine, turned, precision=highest)
    counts = owner_counts[0]
    starts = jnp.cumsum(counts) - counts
    capacity = 2 * rank // (row_count * col_count)
    slots = jnp.arange(capacity, dtype=jnp.int32)
    index = jnp.clip(starts[:, None] + slots[None, :], 0, moment_rows - 1)
    valid = slots[None, :] < counts[:, None]
    outgoing = jnp.where(valid[:, :, None], jnp.take(moved, index, axis=0), f32(0.0))
    owned = lax.all_to_all(outgoing, "col", split_axis=0, concat_axis=2, tiled=True)
    return (new_basis, owned[0])


def solution(mesh):
    in_specs = (P("row", "col"), P("row", None), P("row", "col"), P("row", None))
    out_specs = (P(("row", "col"), None), P(("row", "col"), None))
    return jax.shard_map(body, mesh=mesh, in_specs=in_specs, out_specs=out_specs, check_vma=False)
```

```python
import functools
import itertools

import jax
import jax.numpy as jnp
from jax import lax
from jax.experimental import pallas as pl
from jax.experimental.pallas import tpu as pltpu
from jax.sharding import PartitionSpec as P

highest = lax.Precision.HIGHEST
f32 = jnp.float32
bf16 = jnp.bfloat16
BLOCK = 128
GROUP = 8
PANEL = 64


def leaf_scalars(blk, c):
    head = blk[c:c + GROUP, :]
    cols = [jnp.broadcast_to(head[:, c + j:c + j + 1], (GROUP, BLOCK)) for j in range(GROUP)]
    return {(i, j): jnp.broadcast_to(cols[j][i:i + 1, :], (GROUP, BLOCK)) for j in range(GROUP) for i in range(j + 1)}


def invert_block(blk):
    lanes = lax.broadcasted_iota(jnp.int32, (GROUP, BLOCK), 1)
    subs = lax.broadcasted_iota(jnp.int32, (GROUP, BLOCK), 0)
    later = None
    for g in range(BLOCK // GROUP):
        c = g * GROUP
        end = (c // PANEL + 1) * PANEL
        a = leaf_scalars(blk, c) if later is None else later
        later = leaf_scalars(blk, c + GROUP) if c + GROUP < end else None
        inside = (lanes >= c) & (lanes < c + GROUP)
        head = jnp.where(inside, jnp.where(lanes - c == subs, f32(1), f32(0)), blk[c:c + GROUP, :])
        rows = [jnp.broadcast_to(head[i:i + 1, :], (GROUP, BLOCK)) for i in range(GROUP)]
        low = {}
        scale = []
        for j in range(GROUP):
            scale.append(lax.rsqrt(a[j, j]))
            for k in range(j + 1, GROUP):
                low[j, k] = a[j, k] * scale[j]
            for k in range(j + 1, GROUP):
                for i in range(j + 1, k + 1):
                    a[i, k] = a[i, k] - low[j, i] * low[j, k]
            rows[j] = rows[j] * scale[j]
            for k in range(j + 1, GROUP):
                rows[k] = rows[k] - low[j, k] * rows[j]
        out = rows[0]
        for i in range(1, GROUP):
            out = jnp.where(subs == i, rows[i], out)
        blk[c:c + GROUP, :] = out
        for t in range(g + 1, end // GROUP):
            below = blk[t * GROUP:(t + 1) * GROUP, :]
            col = [jnp.broadcast_to(below[:, c + j:c + j + 1], (GROUP, BLOCK)) for j in range(GROUP)]
            for j in range(GROUP):
                col[j] = col[j] * scale[j]
                for k in range(j + 1, GROUP):
                    col[k] = col[k] - col[j] * low[j, k]
            if t == g + 1:
                for j in range(GROUP):
                    u = [jnp.broadcast_to(col[j][i:i + 1, :], (GROUP, BLOCK)) for i in range(GROUP)]
                    for q in range(GROUP):
                        for p in range(q + 1):
                            later[p, q] = later[p, q] - u[p] * u[q]
            terms = [col[j] * rows[j] for j in range(GROUP)]
            while len(terms) > 1:
                terms = [terms[i] + terms[i + 1] for i in range(0, len(terms), 2)]
            blk[t * GROUP:(t + 1) * GROUP, :] = jnp.where(inside, f32(0), below) - terms[0]
        if c + GROUP == end and end < BLOCK:
            start = end - PANEL
            done = blk[start:end, :]
            lane = lax.broadcasted_iota(jnp.int32, done.shape, 1)
            line = lax.broadcasted_iota(jnp.int32, done.shape, 0) + start
            ahead = (lane >= (line // GROUP + 1) * GROUP) & (lane < end)
            update = mul_t(done, jnp.where(ahead, f32(0), done))[end:, :]
            below = blk[end:, :]
            lane = lax.broadcasted_iota(jnp.int32, below.shape, 1)
            blk[end:, :] = jnp.where((lane >= start) & (lane < end), f32(0), below) - update


vmem = pl.BlockSpec(memory_space=pltpu.VMEM)


def local_params():
    return pltpu.CompilerParams(vmem_limit_bytes=16 * 1024 * 1024)


def mul(a, b):
    return jnp.dot(a, b, precision=highest, preferred_element_type=f32)


def mul_t(a, b):
    return lax.dot_general(a, b, (((0,), (0,)), ((), ())), precision=highest, preferred_element_type=f32)


def eliminate(m_ref, blk):
    n = m_ref.shape[0]
    shape = (BLOCK, BLOCK)
    lower = lax.broadcasted_iota(jnp.int32, shape, 0) >= lax.broadcasted_iota(jnp.int32, shape, 1)
    for o in range(0, n, BLOCK):
        e = o + BLOCK
        blk[...] = m_ref[o:e, o:e]
        invert_block(blk)
        x = jnp.where(lower, blk[...], f32(0))
        m_ref[o:e, o:e] = x
        if o > 0:
            left = mul(x, m_ref[o:e, :o])
            m_ref[o:e, :o] = left
        if e < n:
            right = mul(x, m_ref[o:e, e:])
            m_ref[o:e, e:] = jnp.zeros_like(right)
            m_ref[e:, e:] -= mul_t(right, right)
            m_ref[e:, o:e] = -mul_t(right, x)
            if o > 0:
                m_ref[e:, :o] -= mul_t(right, left)


def factor_kernel(core_ref, own_ref, other_ref, m_ref, blk):
    half = own_ref.shape[1]
    for side in range(2):
        columns = pl.ds(side * half, half)

        @pl.when(core_ref[0] == 0)
        def _(side=side, columns=columns):
            m_ref[:half, columns] = own_ref[side]
            m_ref[half:, columns] = other_ref[side]

        @pl.when(core_ref[0] != 0)
        def _(side=side, columns=columns):
            m_ref[:half, columns] = other_ref[side]
            m_ref[half:, columns] = own_ref[side]
    eliminate(m_ref, blk)


def inverse_factor(core, own, other):
    n = 2 * own.shape[1]
    smem = pl.BlockSpec(memory_space=pltpu.SMEM)
    return pl.pallas_call(
        factor_kernel,
        out_shape=jax.ShapeDtypeStruct((n, n), f32),
        in_specs=[smem, vmem, vmem],
        out_specs=vmem,
        scratch_shapes=[pltpu.VMEM((BLOCK, BLOCK), f32)],
        compiler_params=local_params(),
        cost_estimate=pl.CostEstimate(flops=20_000_000_000, bytes_accessed=8 * n * n, transcendentals=0),
    )(core.reshape(1), own, other)


def parts(value):
    high = value.astype(bf16)
    rest = value - high.astype(f32)
    mid = rest.astype(bf16)
    return high, mid, (rest - mid.astype(f32)).astype(bf16)


def times(left, terms):
    high, mid, low = [jnp.dot(left, term, preferred_element_type=f32) for term in terms]
    return low + mid + high


def pieces_kernel(left_ref, right_ref, *out_refs):
    terms = parts(right_ref[...])
    for d, out_ref in enumerate(out_refs):
        out_ref[...] = times(left_ref[d], terms)


def piece_products(left, right):
    shape = jax.ShapeDtypeStruct((left.shape[1], right.shape[1]), f32)
    flops = 6 * left.size * right.shape[1]
    return pl.pallas_call(
        pieces_kernel,
        out_shape=(shape,) * left.shape[0],
        in_specs=[vmem, vmem],
        out_specs=(vmem,) * left.shape[0],
        compiler_params=local_params(),
        cost_estimate=pl.CostEstimate(flops=flops, bytes_accessed=2 * left.size, transcendentals=0),
    )(left, right)


def setup_kernel(starts_ref, own_ref, basis_ref, slab_ref, turned_ref, *out_refs):
    wide = slab_ref.shape[2]
    terms = parts(basis_ref[...])
    for d in range(4):
        slab_ref[d] = own_ref[:, pl.ds(pl.multiple_of(starts_ref[d], wide), wide)]
        turned_ref[d] = slab_ref[d].T
        out_refs[d][...] = times(turned_ref[d], terms)


def set_up(starts, own, basis):
    rows, wide, rank = own.shape[0], own.shape[1] // 4, basis.shape[1]
    smem = pl.BlockSpec(memory_space=pltpu.SMEM)
    piece = jax.ShapeDtypeStruct((wide, rank), f32)
    slabs = (jax.ShapeDtypeStruct((4, rows, wide), own.dtype), jax.ShapeDtypeStruct((4, wide, rows), own.dtype))
    slab, turned, *pieces = pl.pallas_call(
        setup_kernel,
        out_shape=slabs + (piece,) * 4,
        in_specs=[smem, vmem, vmem],
        out_specs=(vmem,) * 6,
        compiler_params=local_params(),
        cost_estimate=pl.CostEstimate(flops=6 * own.size * rank, bytes_accessed=8 * own.size, transcendentals=0),
    )(starts, own, basis)
    return slab, turned, pieces


def chunk_kernel(first, chunks, *refs):
    left_ref, right_refs, rest = refs[0], refs[1:1 + chunks], refs[1 + chunks:]
    total = None if len(rest) == 1 else rest[0][...]
    for d, right_ref in enumerate(right_refs):
        term = times(left_ref[first + d], parts(right_ref[...]))
        total = term if total is None else total + term
    rest[-1][...] = total


def chunk_products(left, first, rights, total=None):
    shape = jax.ShapeDtypeStruct((left.shape[1], rights[0].shape[1]), f32)
    operands = [left, *rights] + ([] if total is None else [total])
    flops = 6 * len(rights) * left.shape[1] * left.shape[2] * shape.shape[1]
    return pl.pallas_call(
        functools.partial(chunk_kernel, first, len(rights)),
        out_shape=shape,
        in_specs=[vmem] * len(operands),
        out_specs=vmem,
        compiler_params=local_params(),
        cost_estimate=pl.CostEstimate(flops=flops, bytes_accessed=left.size, transcendentals=0),
    )(*operands)


def exact(left, right, dims):
    return lax.dot_general(left, right, (dims, ((), ())), precision=highest)


def after(value, earlier):
    return lax.optimization_barrier((value, earlier))


SIDE = 4


def body(grad, old_basis, old_moments, owner_counts):
    row_count = lax.axis_size("row")
    col_count = lax.axis_size("col")
    chips = col_count // 2
    row = lax.axis_index("row")
    col = lax.axis_index("col")
    core = col % 2
    depth = col // 2
    rank = old_basis.shape[1]
    half = rank // 2
    count = row_count * chips

    def place(x, y, z, c):
        return (x * SIDE + y) * col_count + 2 * z + c

    xs, ys, zs, cs = range(SIDE), range(SIDE), range(chips), range(2)

    groups = dict(
        column=[[place(x, y, z, c) for z in zs] for x in xs for y in ys for c in cs],
        plane=[[place(x, y, z, c) for x in xs for y in ys] for z in zs for c in cs],
        layer=[[place(x, y, z, c) for z in zs for x in xs for y in ys] for c in cs],
    )

    def moved_along(value, step, x_core):
        pairs = []
        for x, y, z, c in itertools.product(xs, ys, zs, cs):
            target = place((x + step) % SIDE, y, z, c) if c == x_core else place(x, (y + step) % SIDE, z, c)
            pairs.append((place(x, y, z, c), target))
        return lax.ppermute(value, ("row", "col"), pairs)

    def line_sum(pieces, x_core):
        far, near, back = [moved_along(pieces[d], d, x_core) for d in (2, 1, 3)]
        return pieces[0] + near + back + far

    def line_gather(value, x_core):
        far, near, back = [moved_along(value, -d, x_core) for d in (2, 1, 3)]
        return [value, near, far, back]

    def exchange(value, kind):
        return lax.all_to_all(value, ("row", "col"), split_axis=0, concat_axis=0, tiled=True, axis_index_groups=groups[kind])

    def swap(value):
        return lax.ppermute(value, "col", [(i, i ^ 1) for i in range(col_count)])

    def both(value, axis):
        other = swap(value)
        first = jnp.where(core == 0, value, other)
        second = jnp.where(core == 0, other, value)
        return jnp.concatenate([first, second], axis=axis)

    def own(value, axis):
        size = value.shape[axis] // 2
        return lax.dynamic_slice_in_dim(value, core * size, size, axis)

    def scatter_sum(value, kind):
        size = len(groups[kind][0])
        return jnp.sum(exchange(value.reshape((size, -1) + value.shape[1:]), kind), axis=0)

    def gather(value, kind):
        size = len(groups[kind][0])
        copies = jnp.broadcast_to(value[None], (size,) + value.shape)
        return exchange(copies, kind).reshape((-1,) + value.shape[1:])

    place_outer = jnp.where(core == 0, row // SIDE, row % SIDE)
    starts = (place_outer + jnp.arange(SIDE)) % SIDE * (grad.shape[1] // SIDE)
    slab, slab_turned, pieces = set_up(starts.astype(jnp.int32), grad, old_basis)

    def image_of(chunk):
        chunks = line_gather(chunk, 0)
        total = chunk_products(slab, 0, chunks[:1])
        total = chunk_products(slab, 2, chunks[2:3], total)
        total = chunk_products(slab, 1, chunks[1:2], total)
        total = chunk_products(slab, 3, chunks[3:], total)
        left, right = total[:, :half], total[:, half:]
        return jnp.where(core == 0, left, right) + swap(jnp.where(core == 0, right, left))

    def layer_sum(value):
        pieces = [value[:, s:s + half].reshape(count // 2, -1, half) for s in (0, half)]
        return jnp.sum(exchange(jnp.concatenate(pieces, axis=0), "layer"), axis=0)

    def joined(value):
        return gather(value, "layer").reshape(2, half, half)

    first = line_sum([line_sum(pieces, 0)] * SIDE, 1)
    image_rows = gather(scatter_sum(image_of(first), "column"), "column")
    image_one = both(image_rows, 1)
    pieces, image_rows = after(piece_products(slab_turned, image_one), image_rows)
    raw = line_sum(pieces, 0)
    width = 2 * half // chips
    mine = lax.dynamic_slice_in_dim(image_rows, depth % 2 * width, width, 1)
    against = lax.dynamic_slice_in_dim(image_one, depth // 2 * half, half, 1)
    cross_one = exact(mine, against, ((0,), (0,))).reshape(row_count, -1, half)
    raw, cross_one = after(raw, jnp.sum(exchange(cross_one, "plane"), axis=0))
    cross_one = joined(cross_one)
    inverse_one = inverse_factor(core, cross_one, swap(cross_one))
    kept, inverse_one = after(raw, inverse_one)
    raw = line_sum([kept] + [raw] * (SIDE - 1), 1)
    projected = exact(raw, inverse_one, ((1,), (1,)))
    cross_old = jnp.dot(inverse_one, both(jnp.concatenate([cross_one[0], cross_one[1]], axis=1), 0), precision=highest)
    image_half, cross_old, old_moments = lax.optimization_barrier((image_of(projected), cross_old, old_moments))
    moments = lax.all_gather(old_moments, "row", axis=0, tiled=True)
    image_half = scatter_sum(image_half, "column")
    image_two = both(image_half, 1)
    cross_two = joined(layer_sum(exact(image_half, image_two, ((0,), (0,)))))
    inverse_two = inverse_factor(core, cross_two, swap(cross_two))
    new_basis = exact(own(image_two, 0), inverse_two, ((1,), (1,)))

    moment_rows = old_moments.shape[0]
    mine = lax.dynamic_slice_in_dim(inverse_two, row * moment_rows, moment_rows, 0)
    rotation = jnp.dot(mine, cross_old, precision=highest)
    moved = jnp.dot(rotation, moments, precision=highest)
    counts = owner_counts[0]
    starts = jnp.cumsum(counts) - counts
    capacity = 2 * rank // (row_count * col_count)
    slots = jnp.arange(capacity, dtype=jnp.int32)
    index = jnp.clip(starts[:, None] + slots[None, :], 0, moment_rows - 1)
    valid = slots[None, :] < counts[:, None]
    outgoing = jnp.where(valid[:, :, None], jnp.take(moved, index, axis=0), f32(0.0))
    owned = lax.all_to_all(outgoing, "col", split_axis=0, concat_axis=2, tiled=True)
    return (new_basis, owned[0])


def solution(mesh):
    in_specs = (P("row", "col"), P("row", None), P("row", "col"), P("row", None))
    out_specs = (P(("row", "col"), None), P(("row", "col"), None))
    return jax.shard_map(body, mesh=mesh, in_specs=in_specs, out_specs=out_specs, check_vma=False)
```

```python
import functools
import itertools

import jax
import jax.numpy as jnp
from jax import lax
from jax.experimental import pallas as pl
from jax.experimental.pallas import tpu as pltpu
from jax.sharding import PartitionSpec as P

highest = lax.Precision.HIGHEST
f32 = jnp.float32
bf16 = jnp.bfloat16
BLOCK = 128
GROUP = 8
PANEL = 64


def leaf_scalars(blk, c):
    head = blk[c:c + GROUP, :]
    cols = [jnp.broadcast_to(head[:, c + j:c + j + 1], (GROUP, BLOCK)) for j in range(GROUP)]
    return {(i, j): jnp.broadcast_to(cols[j][i:i + 1, :], (GROUP, BLOCK)) for j in range(GROUP) for i in range(j + 1)}


def invert_block(blk):
    lanes = lax.broadcasted_iota(jnp.int32, (GROUP, BLOCK), 1)
    subs = lax.broadcasted_iota(jnp.int32, (GROUP, BLOCK), 0)
    later = None
    for g in range(BLOCK // GROUP):
        c = g * GROUP
        end = (c // PANEL + 1) * PANEL
        a = leaf_scalars(blk, c) if later is None else later
        later = leaf_scalars(blk, c + GROUP) if c + GROUP < end else None
        inside = (lanes >= c) & (lanes < c + GROUP)
        head = jnp.where(inside, jnp.where(lanes - c == subs, f32(1), f32(0)), blk[c:c + GROUP, :])
        rows = [jnp.broadcast_to(head[i:i + 1, :], (GROUP, BLOCK)) for i in range(GROUP)]
        low = {}
        scale = []
        for j in range(GROUP):
            scale.append(lax.rsqrt(a[j, j]))
            for k in range(j + 1, GROUP):
                low[j, k] = a[j, k] * scale[j]
            for k in range(j + 1, GROUP):
                for i in range(j + 1, k + 1):
                    a[i, k] = a[i, k] - low[j, i] * low[j, k]
            rows[j] = rows[j] * scale[j]
            for k in range(j + 1, GROUP):
                rows[k] = rows[k] - low[j, k] * rows[j]
        out = rows[0]
        for i in range(1, GROUP):
            out = jnp.where(subs == i, rows[i], out)
        blk[c:c + GROUP, :] = out
        for t in range(g + 1, end // GROUP):
            below = blk[t * GROUP:(t + 1) * GROUP, :]
            col = [jnp.broadcast_to(below[:, c + j:c + j + 1], (GROUP, BLOCK)) for j in range(GROUP)]
            for j in range(GROUP):
                col[j] = col[j] * scale[j]
                for k in range(j + 1, GROUP):
                    col[k] = col[k] - col[j] * low[j, k]
            if t == g + 1:
                for j in range(GROUP):
                    u = [jnp.broadcast_to(col[j][i:i + 1, :], (GROUP, BLOCK)) for i in range(GROUP)]
                    for q in range(GROUP):
                        for p in range(q + 1):
                            later[p, q] = later[p, q] - u[p] * u[q]
            terms = [col[j] * rows[j] for j in range(GROUP)]
            while len(terms) > 1:
                terms = [terms[i] + terms[i + 1] for i in range(0, len(terms), 2)]
            blk[t * GROUP:(t + 1) * GROUP, :] = jnp.where(inside, f32(0), below) - terms[0]
        if c + GROUP == end and end < BLOCK:
            start = end - PANEL
            done = blk[start:end, :]
            lane = lax.broadcasted_iota(jnp.int32, done.shape, 1)
            line = lax.broadcasted_iota(jnp.int32, done.shape, 0) + start
            ahead = (lane >= (line // GROUP + 1) * GROUP) & (lane < end)
            update = mul_t(done, jnp.where(ahead, f32(0), done))[end:, :]
            below = blk[end:, :]
            lane = lax.broadcasted_iota(jnp.int32, below.shape, 1)
            blk[end:, :] = jnp.where((lane >= start) & (lane < end), f32(0), below) - update


vmem = pl.BlockSpec(memory_space=pltpu.VMEM)


def local_params():
    return pltpu.CompilerParams(vmem_limit_bytes=16 * 1024 * 1024)


def mul(a, b):
    return jnp.dot(a, b, precision=highest, preferred_element_type=f32)


def mul_t(a, b):
    return lax.dot_general(a, b, (((0,), (0,)), ((), ())), precision=highest, preferred_element_type=f32)


def eliminate(m_ref, blk):
    n = m_ref.shape[0]
    shape = (BLOCK, BLOCK)
    lower = lax.broadcasted_iota(jnp.int32, shape, 0) >= lax.broadcasted_iota(jnp.int32, shape, 1)
    for o in range(0, n, BLOCK):
        e = o + BLOCK
        blk[...] = m_ref[o:e, o:e]
        invert_block(blk)
        x = jnp.where(lower, blk[...], f32(0))
        m_ref[o:e, o:e] = x
        if o > 0:
            left = mul(x, m_ref[o:e, :o])
            m_ref[o:e, :o] = left
        if e < n:
            right = mul(x, m_ref[o:e, e:])
            m_ref[o:e, e:] = jnp.zeros_like(right)
            m_ref[e:, e:] -= mul_t(right, right)
            m_ref[e:, o:e] = -mul_t(right, x)
            if o > 0:
                m_ref[e:, :o] -= mul_t(right, left)


def factor_kernel(core_ref, own_ref, other_ref, m_ref, blk):
    half = own_ref.shape[1]
    for side in range(2):
        columns = pl.ds(side * half, half)

        @pl.when(core_ref[0] == 0)
        def _(side=side, columns=columns):
            m_ref[:half, columns] = own_ref[side]
            m_ref[half:, columns] = other_ref[side]

        @pl.when(core_ref[0] != 0)
        def _(side=side, columns=columns):
            m_ref[:half, columns] = other_ref[side]
            m_ref[half:, columns] = own_ref[side]
    eliminate(m_ref, blk)


def inverse_factor(core, own, other):
    n = 2 * own.shape[1]
    smem = pl.BlockSpec(memory_space=pltpu.SMEM)
    return pl.pallas_call(
        factor_kernel,
        out_shape=jax.ShapeDtypeStruct((n, n), f32),
        in_specs=[smem, vmem, vmem],
        out_specs=vmem,
        scratch_shapes=[pltpu.VMEM((BLOCK, BLOCK), f32)],
        compiler_params=local_params(),
        cost_estimate=pl.CostEstimate(flops=20_000_000_000, bytes_accessed=8 * n * n, transcendentals=0),
    )(core.reshape(1), own, other)


def parts(value):
    high = value.astype(bf16)
    rest = value - high.astype(f32)
    mid = rest.astype(bf16)
    return high, mid, (rest - mid.astype(f32)).astype(bf16)


def times(left, terms):
    high, mid, low = [jnp.dot(left, term, preferred_element_type=f32) for term in terms]
    return low + mid + high


def pieces_kernel(left_ref, right_ref, *out_refs):
    terms = parts(right_ref[...])
    for d, out_ref in enumerate(out_refs):
        out_ref[...] = times(left_ref[d], terms)


def piece_products(left, right):
    shape = jax.ShapeDtypeStruct((left.shape[1], right.shape[1]), f32)
    flops = 6 * left.size * right.shape[1]
    return pl.pallas_call(
        pieces_kernel,
        out_shape=(shape,) * left.shape[0],
        in_specs=[vmem, vmem],
        out_specs=(vmem,) * left.shape[0],
        compiler_params=local_params(),
        cost_estimate=pl.CostEstimate(flops=flops, bytes_accessed=2 * left.size, transcendentals=0),
    )(left, right)


def setup_kernel(starts_ref, own_ref, basis_ref, slab_ref, turned_ref, *out_refs):
    wide = slab_ref.shape[2]
    terms = parts(basis_ref[...])
    for d in range(4):
        slab_ref[d] = own_ref[:, pl.ds(pl.multiple_of(starts_ref[d], wide), wide)]
        turned_ref[d] = slab_ref[d].T
        out_refs[d][...] = times(turned_ref[d], terms)


def set_up(starts, own, basis):
    rows, wide, rank = own.shape[0], own.shape[1] // 4, basis.shape[1]
    smem = pl.BlockSpec(memory_space=pltpu.SMEM)
    piece = jax.ShapeDtypeStruct((wide, rank), f32)
    slabs = (jax.ShapeDtypeStruct((4, rows, wide), own.dtype), jax.ShapeDtypeStruct((4, wide, rows), own.dtype))
    slab, turned, *pieces = pl.pallas_call(
        setup_kernel,
        out_shape=slabs + (piece,) * 4,
        in_specs=[smem, vmem, vmem],
        out_specs=(vmem,) * 6,
        compiler_params=local_params(),
        cost_estimate=pl.CostEstimate(flops=6 * own.size * rank, bytes_accessed=8 * own.size, transcendentals=0),
    )(starts, own, basis)
    return slab, turned, pieces


def chunk_kernel(first, chunks, *refs):
    left_ref, right_refs, rest = refs[0], refs[1:1 + chunks], refs[1 + chunks:]
    total = None if len(rest) == 1 else rest[0][...]
    for d, right_ref in enumerate(right_refs):
        term = times(left_ref[first + d], parts(right_ref[...]))
        total = term if total is None else total + term
    rest[-1][...] = total


def chunk_products(left, first, rights, total=None):
    shape = jax.ShapeDtypeStruct((left.shape[1], rights[0].shape[1]), f32)
    operands = [left, *rights] + ([] if total is None else [total])
    flops = 6 * len(rights) * left.shape[1] * left.shape[2] * shape.shape[1]
    return pl.pallas_call(
        functools.partial(chunk_kernel, first, len(rights)),
        out_shape=shape,
        in_specs=[vmem] * len(operands),
        out_specs=vmem,
        compiler_params=local_params(),
        cost_estimate=pl.CostEstimate(flops=flops, bytes_accessed=left.size, transcendentals=0),
    )(*operands)


def exact(left, right, dims):
    return lax.dot_general(left, right, (dims, ((), ())), precision=highest)


def after(value, earlier):
    return lax.optimization_barrier((value, earlier))


SIDE = 4


def body(grad, old_basis, old_moments, owner_counts):
    row_count = lax.axis_size("row")
    col_count = lax.axis_size("col")
    chips = col_count // 2
    row = lax.axis_index("row")
    col = lax.axis_index("col")
    core = col % 2
    depth = col // 2
    rank = old_basis.shape[1]
    half = rank // 2
    count = row_count * chips

    def place(x, y, z, c):
        return (x * SIDE + y) * col_count + 2 * z + c

    xs, ys, zs, cs = range(SIDE), range(SIDE), range(chips), range(2)

    groups = dict(
        column=[[place(x, y, z, c) for z in zs] for x in xs for y in ys for c in cs],
        plane=[[place(x, y, z, c) for x in xs for y in ys] for z in zs for c in cs],
        layer=[[place(x, y, z, c) for z in zs for x in xs for y in ys] for c in cs],
    )

    def moved_along(value, step, x_core):
        pairs = []
        for x, y, z, c in itertools.product(xs, ys, zs, cs):
            target = place((x + step) % SIDE, y, z, c) if c == x_core else place(x, (y + step) % SIDE, z, c)
            pairs.append((place(x, y, z, c), target))
        return lax.ppermute(value, ("row", "col"), pairs)

    def line_sum(pieces, x_core):
        far, near, back = [moved_along(pieces[d], d, x_core) for d in (2, 1, 3)]
        return pieces[0] + near + back + far

    def line_gather(value, x_core):
        far, near, back = [moved_along(value, -d, x_core) for d in (2, 1, 3)]
        return [value, near, far, back]

    def exchange(value, kind):
        return lax.all_to_all(value, ("row", "col"), split_axis=0, concat_axis=0, tiled=True, axis_index_groups=groups[kind])

    def swap(value):
        return lax.ppermute(value, "col", [(i, i ^ 1) for i in range(col_count)])

    def both(value, axis):
        other = swap(value)
        first = jnp.where(core == 0, value, other)
        second = jnp.where(core == 0, other, value)
        return jnp.concatenate([first, second], axis=axis)

    def own(value, axis):
        size = value.shape[axis] // 2
        return lax.dynamic_slice_in_dim(value, core * size, size, axis)

    def scatter_sum(value, kind):
        size = len(groups[kind][0])
        return jnp.sum(exchange(value.reshape((size, -1) + value.shape[1:]), kind), axis=0)

    def gather(value, kind):
        size = len(groups[kind][0])
        copies = jnp.broadcast_to(value[None], (size,) + value.shape)
        return exchange(copies, kind).reshape((-1,) + value.shape[1:])

    place_outer = jnp.where(core == 0, row // SIDE, row % SIDE)
    starts = (place_outer + jnp.arange(SIDE)) % SIDE * (grad.shape[1] // SIDE)
    slab, slab_turned, pieces = set_up(starts.astype(jnp.int32), grad, old_basis)

    def image_of(chunk):
        chunks = line_gather(chunk, 0)
        total = chunk_products(slab, 0, chunks[:1])
        total = chunk_products(slab, 2, chunks[2:3], total)
        total = chunk_products(slab, 1, chunks[1:2], total)
        total = chunk_products(slab, 3, chunks[3:], total)
        left, right = total[:, :half], total[:, half:]
        return jnp.where(core == 0, left, right) + swap(jnp.where(core == 0, right, left))

    def layer_sum(value):
        pieces = [value[:, s:s + half].reshape(count // 2, -1, half) for s in (0, half)]
        return jnp.sum(exchange(jnp.concatenate(pieces, axis=0), "layer"), axis=0)

    def joined(value):
        return gather(value, "layer").reshape(2, half, half)

    first = line_sum([line_sum(pieces, 0)] * SIDE, 1)
    image_rows, old_moments = after(image_of(first), old_moments)
    moments = lax.all_gather(old_moments, "row", axis=0, tiled=True)
    image_rows = gather(scatter_sum(image_rows, "column"), "column")
    image_one = both(image_rows, 1)
    pieces, image_rows = after(piece_products(slab_turned, image_one), image_rows)
    raw = line_sum(pieces, 0)
    width = 2 * half // chips
    mine = lax.dynamic_slice_in_dim(image_rows, depth % 2 * width, width, 1)
    against = lax.dynamic_slice_in_dim(image_one, depth // 2 * half, half, 1)
    cross_one = exact(mine, against, ((0,), (0,))).reshape(row_count, -1, half)
    cross_one = jnp.sum(exchange(cross_one, "plane"), axis=0)
    raw, cross_one, moments = lax.optimization_barrier((raw, cross_one, moments))
    cross_one = joined(cross_one)
    inverse_one = inverse_factor(core, cross_one, swap(cross_one))
    kept, inverse_one = after(raw, inverse_one)
    raw = line_sum([kept] + [raw] * (SIDE - 1), 1)
    projected = exact(raw, inverse_one, ((1,), (1,)))
    cross_old = jnp.dot(inverse_one, both(jnp.concatenate([cross_one[0], cross_one[1]], axis=1), 0), precision=highest)
    image_half, cross_old = after(image_of(projected), cross_old)
    image_half = scatter_sum(image_half, "column")
    image_two = both(image_half, 1)
    cross_two = joined(layer_sum(exact(image_half, image_two, ((0,), (0,)))))
    inverse_two = inverse_factor(core, cross_two, swap(cross_two))
    new_basis = exact(own(image_two, 0), inverse_two, ((1,), (1,)))

    moment_rows = old_moments.shape[0]
    mine = lax.dynamic_slice_in_dim(inverse_two, row * moment_rows, moment_rows, 0)
    rotation = jnp.dot(mine, cross_old, precision=highest)
    moved = jnp.dot(rotation, moments, precision=highest)
    counts = owner_counts[0]
    starts = jnp.cumsum(counts) - counts
    capacity = 2 * rank // (row_count * col_count)
    slots = jnp.arange(capacity, dtype=jnp.int32)
    index = jnp.clip(starts[:, None] + slots[None, :], 0, moment_rows - 1)
    valid = slots[None, :] < counts[:, None]
    outgoing = jnp.where(valid[:, :, None], jnp.take(moved, index, axis=0), f32(0.0))
    owned = lax.all_to_all(outgoing, "col", split_axis=0, concat_axis=2, tiled=True)
    return (new_basis, owned[0])


def solution(mesh):
    in_specs = (P("row", "col"), P("row", None), P("row", "col"), P("row", None))
    out_specs = (P(("row", "col"), None), P(("row", "col"), None))
    return jax.shard_map(body, mesh=mesh, in_specs=in_specs, out_specs=out_specs, check_vma=False)
```
